256 devices in a mesh: row: 16 (over y, x_hi, core), col: 16 (over x_lo, z).
Axes of the slice: x: 4 (x_hi: 2, x_lo: 2; x = x_hi * 2 + x_lo), y: 4, z: 8, core: 2. Of those that a mesh axis runs over, the one named last changes fastest.
Arguments:
- tokens: bfloat16 [1024, 8192], P('col', 'row'), may hold values from -6 to 6
- cotangent: bfloat16 [1024, 8192], P('col', 'row'), may hold values from -6 to 6
- gate_weight: bfloat16 [8192, 16384], P('row', 'col'), may hold values from -0.0625 to 0.0625
- up_weight: bfloat16 [8192, 16384], P('row', 'col'), may hold values from -0.0625 to 0.0625
- down_weight: bfloat16 [16384, 8192], P('col', 'row'), may hold values from -0.046875 to 0.046875
Outputs:
- token_grad: float32 [1024, 8192], P('col', 'row')
- gate_grad: float32 [8192, 16384], P('row', 'col')
- up_grad: float32 [8192, 16384], P('row', 'col')
- down_grad: float32 [16384, 8192], P('col', 'row')
The draws below stay inside these ranges and needn't reach their ends.
All inputs are finite; a program needn't handle non-finite values.
Results may differ from the reference program's by a relative error of at most 0.0029.
Values may be sent and summed in bfloat16 or wider, within the bound.
No kernel may reach another device: no remote copies, remote signals or barrier semaphores. Data moves between devices by JAX's collectives and lax.ppermute only.
A program may use at most 64 MiB of HBM per device.

```python
import jax
import jax.numpy as jnp

D = 8192
FF = 16384
TOKENS = 1024


def levels(own_key, shape, pieces, low, top_value):
    factor_of, own = 1.0, jax.random.fold_in(own_key, 6)
    for axis_at, parts in pieces:
        draws = jnp.exp(jax.random.uniform(jax.random.fold_in(own, axis_at), (parts,), jnp.float32, low / len(pieces), top_value / len(pieces)))
        factor_of = factor_of * jnp.repeat(draws, shape[axis_at] // parts).reshape([-1 if axis == axis_at else 1 for axis in range(len(shape))])
    return factor_of


def noise(rng, shape, width, limit, split=(), held_as=jnp.bfloat16):
    gain = levels(rng, shape, split, -0.22, 0.18) if split else 1.0
    entries = jax.random.normal(rng, shape, jnp.float32) * width * gain
    return jnp.minimum(jnp.maximum(entries, -limit), limit).astype(held_as)


def setup_inputs(seed: int = 0) -> dict:
    streams_of = jax.random.split(jax.random.key(seed), 6)
    tokens = noise(streams_of[0], (TOKENS, D), 1.0, 6.0, ((0, 16), (1, 16)))
    cotangent = noise(streams_of[1], (TOKENS, D), 1.0, 6.0, ((0, 16), (1, 16)))
    gate_weight = noise(streams_of[2], (D, FF), D ** -0.5, 0.0625, ((0, 16), (1, 16)))
    up_weight = noise(streams_of[3], (D, FF), D ** -0.5, 0.0625, ((0, 16), (1, 16)))
    down_weight = noise(streams_of[4], (FF, D), FF ** -0.5, 0.046875, ((0, 16), (1, 16)))
    return {"tokens": tokens, "cotangent": cotangent, "gate_weight": gate_weight, "up_weight": up_weight, "down_weight": down_weight}


def reference(tokens, cotangent, gate_weight, up_weight, down_weight):
    gate = jnp.dot(tokens, gate_weight, preferred_element_type=jnp.float32)
    up = jnp.dot(tokens, up_weight, preferred_element_type=jnp.float32)
    hidden_grad = jnp.dot(cotangent, down_weight.T, preferred_element_type=jnp.float32)
    sigma = jax.nn.sigmoid(gate)
    silu_gate = gate * sigma
    hidden = (silu_gate * up).astype(jnp.bfloat16)
    pre_gate_grad = (hidden_grad * up * sigma * (1.0 + gate * (1.0 - sigma))).astype(jnp.bfloat16)
    pre_up_grad = (hidden_grad * silu_gate).astype(jnp.bfloat16)
    down_grad = jnp.dot(hidden.T, cotangent, preferred_element_type=jnp.float32)
    gate_grad = jnp.dot(tokens.T, pre_gate_grad, preferred_element_type=jnp.float32)
    up_grad = jnp.dot(tokens.T, pre_up_grad, preferred_element_type=jnp.float32)
    token_grad = jnp.dot(pre_gate_grad, gate_weight.T, preferred_element_type=jnp.float32) + jnp.dot(pre_up_grad, up_weight.T, preferred_element_type=jnp.float32)
    return token_grad, gate_grad, up_grad, down_grad
```

```python
import jax
import jax.numpy as jnp
from jax import lax
from jax.experimental import pallas as pl
from jax.experimental.pallas import tpu as pltpu
from jax.sharding import Mesh, PartitionSpec as P

BF = jnp.bfloat16
F32 = jnp.float32
SIZES = {"y": 4, "h": 2, "c": 2, "l": 2, "z": 8}


def hop(x, axis, step=1):
    n = SIZES[axis]
    return lax.ppermute(x, axis, [(i, (i + step) % n) for i in range(n)])


def ring(x):
    up, down = [x], [x]
    for _ in range(3):
        up.append(hop(up[-1], "z", 1))
        down.append(hop(down[-1], "z", -1))
    half = x.shape[0] // 2
    far = jnp.concatenate([hop(up[3][:half], "z", 1), hop(down[3][half:], "z", -1)])
    return up + [far] + down[:0:-1]


def encode(v):
    v = v * 16.0
    s = v * jnp.abs(v)
    t = v * v
    return (s * t * (t * t)).astype(BF)


def decode(code):
    y = code.astype(F32)
    q = lax.rsqrt(lax.rsqrt(jnp.maximum(jnp.abs(y), 1e-37)))
    t = q * lax.rsqrt(q) * (1.0 / 16.0)
    return jnp.where(y == 0.0, 0.0, jnp.where(y < 0.0, -t, t))


def place_kernel(spot_ref, *refs):
    blocks, (feat, grad, sems) = refs[:16], refs[16:]
    copies = []
    for i in range(16):
        start = pl.multiple_of(spot_ref[i] * 64, 64)
        for j, out in enumerate((feat, grad)):
            copies.append(
                pltpu.make_async_copy(
                    blocks[i].at[pl.ds(64 * j, 64)],
                    out.at[pl.ds(start, 64)],
                    sems.at[2 * i + j],
                )
            )
    for copy in copies:
        copy.start()
    for copy in copies:
        copy.wait()


def place(blocks, spots):
    shape = jax.ShapeDtypeStruct((1024, 512), BF)
    return pl.pallas_call(
        place_kernel,
        out_shape=(shape, shape),
        in_specs=[pl.BlockSpec(memory_space=pltpu.SMEM)]
        + [pl.BlockSpec(memory_space=pl.ANY)] * 16,
        out_specs=[pl.BlockSpec(memory_space=pl.ANY)] * 2,
        scratch_shapes=[pltpu.SemaphoreType.DMA((32,))],
        name="place",
    )(spots, *blocks)


def dot_nn(a, b):
    return jnp.dot(a, b, preferred_element_type=F32)


def dot_nt(a, b):
    return lax.dot_general(a, b, (((1,), (1,)), ((), ())), preferred_element_type=F32)


def dot_tn(a, b):
    return lax.dot_general(a, b, (((0,), (0,)), ((), ())), preferred_element_type=F32)


def shards(tokens, cotangent, gate_weight, up_weight, down_weight):
    core, near, z = lax.axis_index("c"), lax.axis_index("l"), lax.axis_index("z")
    mine = jnp.concatenate([tokens, cotangent])
    blocks = ring(mine) + ring(hop(mine, "l"))
    where = jnp.arange(16)
    from_l, from_z = (near + where // 8) % 2, (z - where % 8) % 8
    spots = ((from_l + core) % 2) * 8 + from_z
    features, grads = place(blocks, spots.astype(jnp.int32))

    def sums(half):
        f, g = features[half], grads[half]
        return [dot_nn(f, gate_weight), dot_nn(f, up_weight), dot_nt(g, down_weight)]

    keep, send = slice(0, 512), slice(512, 1024)
    theirs = hop(jnp.concatenate([encode(v) for v in sums(send)], axis=1), "c")
    both = jnp.concatenate(sums(keep), axis=1) + decode(theirs)
    parts = lax.all_to_all(encode(both), ("y", "h"), 0, 0, tiled=True)
    total = decode(parts).reshape(8, 64, 3072).sum(0)
    gate, up, hidden_grad = total[:, :1024], total[:, 1024:2048], total[:, 2048:]
    sigma = jax.nn.sigmoid(gate)
    silu_gate = gate * sigma
    hidden = (silu_gate * up).astype(BF)
    pre_gate = (hidden_grad * up * sigma * (1.0 + gate * (1.0 - sigma))).astype(BF)
    pre_up = (hidden_grad * silu_gate).astype(BF)
    own = jnp.concatenate([hidden, pre_gate, pre_up], axis=1)
    ours = lax.all_to_all(
        jnp.broadcast_to(own[None], (8, 64, 3072)).reshape(512, 3072), ("y", "h"), 0, 0, tiled=True
    )
    every = jnp.concatenate([ours, hop(ours, "c")])
    hidden_all, gate_all, up_all = every[:, :1024], every[:, 1024:2048], every[:, 2048:]
    token_part = (dot_nt(gate_all, gate_weight) + dot_nt(up_all, up_weight)).astype(BF)
    twice = jnp.concatenate([token_part, token_part[:512]])
    token_part = lax.dynamic_slice(twice, (core * 512, 0), (1024, 512))
    token_parts = lax.all_to_all(token_part, ("l", "z"), 0, 0, tiled=True)
    token_grad = token_parts.astype(F32).reshape(16, 64, 512).sum(0)
    return (
        token_grad,
        dot_tn(features, gate_all),
        dot_tn(features, up_all),
        dot_tn(hidden_all, grads),
    )


def solution(mesh):
    fine = Mesh(mesh.devices.reshape(4, 2, 2, 2, 8), ("y", "h", "c", "l", "z"))
    row, col = ("y", "h", "c"), ("l", "z")
    return jax.shard_map(
        shards,
        mesh=fine,
        in_specs=(P(col, row), P(col, row), P(row, col), P(row, col), P(col, row)),
        out_specs=(P(col, row), P(row, col), P(row, col), P(col, row)),
        check_vma=False,
    )
```

```python
import jax
import jax.numpy as jnp
from jax import lax
from jax.sharding import Mesh, PartitionSpec as P

BF = jnp.bfloat16
F16 = jnp.float16
F32 = jnp.float32
SIZES = {"y": 4, "h": 2, "c": 2, "l": 2, "z": 8}


def hop(x, axis, step=1):
    n = SIZES[axis]
    return lax.ppermute(x, axis, [(i, (i + step) % n) for i in range(n)])


def swap(x, axis):
    return lax.all_to_all(x, axis, 0, 0, tiled=True)


def ring(x):
    up, down = [x], [x]
    for _ in range(3):
        up.append(hop(up[-1], "z", 1))
        down.append(hop(down[-1], "z", -1))
    half = x.shape[0] // 2
    far = jnp.concatenate([hop(up[3][:half], "z", 1), hop(down[3][half:], "z", -1)])
    return up + [far] + down[:0:-1]


def encode(v):
    return (v * 16.0).astype(F16)


def decode(v):
    return v.astype(F32) * (1.0 / 16.0)


def dot_nn(a, b):
    return jnp.dot(a, b, preferred_element_type=F32)


def dot_nt(a, b):
    return lax.dot_general(a, b, (((1,), (1,)), ((), ())), preferred_element_type=F32)


def dot_tn(a, b):
    return lax.dot_general(a, b, (((0,), (0,)), ((), ())), preferred_element_type=F32)


def select(order, x):
    hot = (order[:, None] == jnp.arange(x.shape[0])[None, :]).astype(BF)
    return dot_nn(hot, x).astype(BF)


def restore(order, x):
    hot = (order[:, None] == jnp.arange(x.shape[0])[None, :]).astype(BF)
    return dot_tn(hot, x).astype(BF)


def shards(tokens, cotangent, gate_weight, up_weight, down_weight):
    y, h, c, l, z = (lax.axis_index(a) for a in ("y", "h", "c", "l", "z"))

    i = jnp.arange(512)
    d_c, d_8, low = i // 256, (i // 32) % 8, i % 32

    def rows(d_y, d_h):
        return (((c + d_c) % 2) * 8 + ((y + d_y) % 4) * 2 + (h + d_h) % 2) * 32 + low

    order_a = rows(d_8 % 4, d_8 // 4)
    order_b = rows(d_8 // 2, d_8 % 2)
    order_near_a, order_near_b = (
        ((z - order // 64) % 8) * 64 + order % 64 for order in (order_a, order_b)
    )

    def sums(f, g):
        return jnp.concatenate(
            [dot_nn(f, gate_weight), dot_nn(f, up_weight), dot_nt(g, down_weight)], axis=1
        )

    def chip_sums(f, g):
        theirs = hop(encode(sums(f[256:], g[256:])), "c")
        return sums(f[:256], g[:256]) + decode(theirs)

    def activate(total):
        gate, up, hidden_grad = total[:, :1024], total[:, 1024:2048], total[:, 2048:]
        sigma = jax.nn.sigmoid(gate)
        silu_gate = gate * sigma
        hidden = (silu_gate * up).astype(BF)
        pre_gate = (hidden_grad * up * sigma * (1.0 + gate * (1.0 - sigma))).astype(BF)
        pre_up = (hidden_grad * silu_gate).astype(BF)
        return hidden, jnp.concatenate([pre_gate, pre_up], axis=1)

    def send_y(x):
        return [hop(encode(x(d)), "y", d) for d in (1, 2, 3)]

    def send_h(x):
        return [hop(encode(x(1)), "h")]

    def add(own, others):
        return own + sum(decode(other) for other in others)

    def spread_y(x):
        return [hop(x, "y", -d) for d in (1, 2, 3)]

    def spread_h(x):
        return [hop(x, "h")]

    together = lax.optimization_barrier

    def token_part(x):
        return (dot_nt(x[:, :1024], gate_weight) + dot_nt(x[:, 1024:], up_weight)).astype(BF)

    mine = jnp.concatenate([tokens, cotangent])
    near, far = ring(mine), ring(hop(mine, "l"))
    f_a = select(order_near_a, jnp.concatenate([b[:64] for b in near]))
    g_a = select(order_near_a, jnp.concatenate([b[64:] for b in near]))
    f_b = select(order_near_b, jnp.concatenate([b[:64] for b in far]))
    g_b = select(order_near_b, jnp.concatenate([b[64:] for b in far]))

    chip_a = chip_sums(f_a, g_a).reshape(2, 4, 32, 3072)
    chip_b = chip_sums(f_b, g_b).reshape(4, 2, 32, 3072)
    chip_a, chip_b = together((chip_a, chip_b))
    from_y, from_h = together((send_y(lambda d: chip_a[:, d]), send_h(lambda d: chip_b[:, d])))
    pair_a, line_b = together((add(chip_a[:, 0], from_y), add(chip_b[:, 0], from_h)))
    from_h, from_y = together((send_h(lambda d: pair_a[d]), send_y(lambda d: line_b[d])))
    hidden_a, pre_a = activate(add(pair_a[0], from_h))
    hidden_b, pre_b = activate(add(line_b[0], from_y))

    def gather(a, b):
        from_y, from_h = together((spread_y(a), spread_h(b)))
        a, b = together((jnp.concatenate([a] + from_y), jnp.concatenate([b] + from_h)))
        from_h, from_y = together((spread_h(a), spread_y(b)))
        return jnp.concatenate([a] + from_h), jnp.concatenate([b] + from_y)

    pre_a, pre_b, hidden_a, hidden_b = together((*gather(pre_a, pre_b), hidden_a, hidden_b))
    other_b = hop(pre_b, "c")
    other_a = hop(pre_a, "c")
    part_a = restore(order_a, jnp.concatenate([token_part(pre_a), token_part(other_a)]))
    part_b = restore(order_b, jnp.concatenate([token_part(pre_b), token_part(other_b)]))
    part = jnp.where(l == 0, jnp.concatenate([part_a, part_b]), jnp.concatenate([part_b, part_a]))
    token_grad = swap(part, ("l", "z")).astype(F32).reshape(16, 64, 512).sum(0)

    hidden_a, hidden_b = gather(hidden_a, hidden_b)
    hidden_all = jnp.concatenate([hidden_a, hop(hidden_a, "c"), hidden_b, hop(hidden_b, "c")])
    features = jnp.concatenate([f_a, f_b])
    grads = jnp.concatenate([g_a, g_b])
    pre_all = jnp.concatenate([pre_a, other_a, pre_b, other_b])
    gate_grad = dot_tn(features, pre_all[:, :1024])
    up_grad = dot_tn(features, pre_all[:, 1024:])
    down_grad = dot_tn(hidden_all, grads)
    return token_grad, gate_grad, up_grad, down_grad


def solution(mesh):
    fine = Mesh(mesh.devices.reshape(4, 2, 2, 2, 8), ("y", "h", "c", "l", "z"))
    row, col = ("y", "h", "c"), ("l", "z")
    return jax.shard_map(
        shards,
        mesh=fine,
        in_specs=(P(col, row), P(col, row), P(row, col), P(row, col), P(col, row)),
        out_specs=(P(col, row), P(row, col), P(row, col), P(col, row)),
        check_vma=False,
    )
```

```python
import jax
import jax.numpy as jnp
from jax import lax
from jax.sharding import Mesh, PartitionSpec as P

BF = jnp.bfloat16
F16 = jnp.float16
F32 = jnp.float32
SIZES = {"y": 4, "h": 2, "c": 2, "l": 2, "z": 8}


def hop(x, axis, step=1):
    n = SIZES[axis]
    return lax.ppermute(x, axis, [(i, (i + step) % n) for i in range(n)])


def swap(x, axis):
    return lax.all_to_all(x, axis, 0, 0, tiled=True)


def ring(x):
    up, down = [x], [x]
    for _ in range(3):
        up.append(hop(up[-1], "z", 1))
        down.append(hop(down[-1], "z", -1))
    half = x.shape[0] // 2
    last = [hop(up[3][:half], "z", 1), hop(down[3][half:], "z", -1)]
    return up, last, down


def encode(v):
    return (v * 16.0).astype(F16)


def decode(v):
    return v.astype(F32) * (1.0 / 16.0)


def dot_nn(a, b):
    return jnp.dot(a, b, preferred_element_type=F32)


def dot_nt(a, b):
    return lax.dot_general(a, b, (((1,), (1,)), ((), ())), preferred_element_type=F32)


def dot_tn(a, b):
    return lax.dot_general(a, b, (((0,), (0,)), ((), ())), preferred_element_type=F32)


def select(order, x):
    hot = (order[:, None] == jnp.arange(x.shape[0])[None, :]).astype(BF)
    return dot_nn(hot, x).astype(BF)


def restore(order, x):
    hot = (order[:, None] == jnp.arange(x.shape[0])[None, :]).astype(BF)
    return dot_tn(hot, x).astype(BF)


def shards(tokens, cotangent, gate_weight, up_weight, down_weight):
    y, h, c, l, z = (lax.axis_index(a) for a in ("y", "h", "c", "l", "z"))

    i = jnp.arange(512)
    d_c, d_8, low = i // 256, (i // 32) % 8, i % 32

    def rows(d_y, d_h):
        return (((c + d_c) % 2) * 8 + ((y + d_y) % 4) * 2 + (h + d_h) % 2) * 32 + low

    order_a = rows(d_8 % 4, d_8 // 4)
    order_b = rows(d_8 // 2, d_8 % 2)
    order_near_a, order_near_b = (
        ((z - order // 64) % 8) * 64 + order % 64 for order in (order_a, order_b)
    )

    def sums(f, g):
        return jnp.concatenate(
            [dot_nn(f, gate_weight), dot_nn(f, up_weight), dot_nt(g, down_weight)], axis=1
        )

    def chip_sums(f, g):
        theirs = hop(encode(sums(f[256:], g[256:])), "c")
        return sums(f[:256], g[:256]) + decode(theirs)

    def activate(total):
        gate, up, hidden_grad = total[:, :1024], total[:, 1024:2048], total[:, 2048:]
        sigma = jax.nn.sigmoid(gate)
        silu_gate = gate * sigma
        hidden = (silu_gate * up).astype(BF)
        pre_gate = (hidden_grad * up * sigma * (1.0 + gate * (1.0 - sigma))).astype(BF)
        pre_up = (hidden_grad * silu_gate).astype(BF)
        return jnp.concatenate([pre_gate, pre_up, hidden], axis=1)

    def send_y(x):
        return [hop(encode(x(d)), "y", d) for d in (2, 1, 3)]

    def send_h(x):
        return [hop(encode(x(1)), "h")]

    def add(own, others):
        return own + sum(decode(other) for other in others)

    def spread_y(x):
        return [hop(x, "y", -d) for d in (1, 2, 3)]

    def spread_h(x):
        return [hop(x, "h")]

    together = lax.optimization_barrier

    def token_part(x):
        return dot_nt(x[:, :1024], gate_weight) + dot_nt(x[:, 1024:2048], up_weight)

    mine = lax.optimization_barrier(jnp.concatenate([tokens, cotangent]))
    near, far = lax.optimization_barrier((ring(mine), ring(hop(mine, "l"))))
    near, far = ([*up, jnp.concatenate(last), *down[:0:-1]] for up, last, down in (near, far))
    f_a = select(order_near_a, jnp.concatenate([b[:64] for b in near]))
    g_a = select(order_near_a, jnp.concatenate([b[64:] for b in near]))
    f_b = select(order_near_b, jnp.concatenate([b[:64] for b in far]))
    g_b = select(order_near_b, jnp.concatenate([b[64:] for b in far]))

    chip_a = chip_sums(f_a, g_a).reshape(2, 4, 32, 3072)
    chip_b = chip_sums(f_b, g_b).reshape(4, 2, 32, 3072)
    chip_a, chip_b = together((chip_a, chip_b))
    from_y, from_h = together((send_y(lambda d: chip_a[:, d]), send_h(lambda d: chip_b[:, d])))
    pair_a, line_b = together((add(chip_a[:, 0], from_y), add(chip_b[:, 0], from_h)))
    features, grads = jnp.concatenate([f_a, f_b]), jnp.concatenate([g_a, g_b])
    features, grads = together((features, grads))
    from_h, from_y = together((send_h(lambda d: pair_a[d]), send_y(lambda d: line_b[d])))
    act_a = activate(add(pair_a[0], from_h))
    act_b = activate(add(line_b[0], from_y))

    from_y, from_h = together((spread_y(act_a), spread_h(act_b)))
    act_a, act_b = together((jnp.concatenate([act_a] + from_y), jnp.concatenate([act_b] + from_h)))
    from_h, from_y = together((spread_h(act_a), spread_y(act_b)))
    act_a, act_b = together((jnp.concatenate([act_a] + from_h), jnp.concatenate([act_b] + from_y)))
    other_b = hop(act_b, "c")
    other_a = hop(act_a, "c")

    far_part = jnp.concatenate([token_part(act_b).astype(BF), token_part(other_b).astype(BF)])
    far_part = far_part.reshape(2, 4, 2, 32, 512).swapaxes(1, 2).reshape(512, 512)
    near_part = jnp.concatenate([token_part(act_a), token_part(other_a)])
    near_part = (near_part + hop(far_part, "l").astype(F32)).astype(BF)
    token_grad = swap(restore(order_a, near_part), "z").astype(F32).reshape(8, 64, 512).sum(0)

    every = jnp.concatenate([act_a, other_a, act_b, other_b])
    return (
        token_grad,
        dot_tn(features, every[:, :1024]),
        dot_tn(features, every[:, 1024:2048]),
        dot_tn(every[:, 2048:], grads),
    )


def solution(mesh):
    fine = Mesh(mesh.devices.reshape(4, 2, 2, 2, 8), ("y", "h", "c", "l", "z"))
    row, col = ("y", "h", "c"), ("l", "z")
    return jax.shard_map(
        shards,
        mesh=fine,
        in_specs=(P(col, row), P(col, row), P(row, col), P(row, col), P(col, row)),
        out_specs=(P(col, row), P(row, col), P(row, col), P(col, row)),
        check_vma=False,
    )
```

```python
import jax
import jax.numpy as jnp
from jax import lax
from jax.sharding import Mesh, PartitionSpec as P

BF = jnp.bfloat16
F16 = jnp.float16
F32 = jnp.float32
SIZES = {"y": 4, "h": 2, "c": 2, "l": 2, "z": 8}


def hop(x, axis, step=1):
    n = SIZES[axis]
    return lax.ppermute(x, axis, [(i, (i + step) % n) for i in range(n)])


def swap(x, axis):
    return lax.all_to_all(x, axis, 0, 0, tiled=True)


def ring(x):
    up, down = [x], [x]
    for _ in range(3):
        up.append(hop(up[-1], "z", 1))
        down.append(hop(down[-1], "z", -1))
    half = x.shape[0] // 2
    last = [hop(up[3][:half], "z", 1), hop(down[3][half:], "z", -1)]
    return up, last, down


def encode(v):
    return (v * 16.0).astype(F16)


def decode(v):
    return v.astype(F32) * (1.0 / 16.0)


def dot_nn(a, b):
    return jnp.dot(a, b, preferred_element_type=F32)


def dot_nt(a, b):
    return lax.dot_general(a, b, (((1,), (1,)), ((), ())), preferred_element_type=F32)


def dot_tn(a, b):
    return lax.dot_general(a, b, (((0,), (0,)), ((), ())), preferred_element_type=F32)


def select(order, x):
    hot = (order[:, None] == jnp.arange(x.shape[0])[None, :]).astype(BF)
    return dot_nn(hot, x).astype(BF)


def restore(order, x):
    hot = (order[:, None] == jnp.arange(x.shape[0])[None, :]).astype(BF)
    return dot_tn(hot, x).astype(BF)


def shards(tokens, cotangent, gate_weight, up_weight, down_weight):
    y, h, c, z = (lax.axis_index(a) for a in ("y", "h", "c", "z"))

    i = jnp.arange(256)
    block, low = i // 32, i % 32
    chips_a = (y + block % 4) % 4 * 2 + (h + block // 4) % 2
    chips_b = (y + block // 2) % 4 * 2 + (h + block % 2) % 2

    order_a, order_b = (
        jnp.concatenate([(z - chips) % 8 * 64 + core * 32 + low for core in (c, 1 - c)])
        for chips in (chips_a, chips_b)
    )
    place_a = jnp.concatenate([chips_a * 64 + core * 32 + low for core in (c, 1 - c)])

    gate_other, up_other, down_other = (hop(w, "c") for w in (gate_weight, up_weight, down_weight))

    def sums(f, g, f_other, g_other):
        return jnp.concatenate(
            [
                dot_nn(f, gate_weight) + dot_nn(f_other, gate_other),
                dot_nn(f, up_weight) + dot_nn(f_other, up_other),
                dot_nt(g, down_weight) + dot_nt(g_other, down_other),
            ],
            axis=1,
        )

    def activate(total):
        gate, up, hidden_grad = total[:, :1024], total[:, 1024:2048], total[:, 2048:]
        sigma = jax.nn.sigmoid(gate)
        silu_gate = gate * sigma
        hidden = (silu_gate * up).astype(BF)
        pre_gate = (hidden_grad * up * sigma * (1.0 + gate * (1.0 - sigma))).astype(BF)
        pre_up = (hidden_grad * silu_gate).astype(BF)
        return jnp.concatenate([pre_gate, pre_up, hidden], axis=1)

    def send_y(x):
        return [hop(encode(x(d)), "y", d) for d in (2, 1, 3)]

    def send_h(x):
        return [hop(encode(x(1)), "h")]

    def add(own, others):
        return own + sum(decode(other) for other in others)

    def spread_y(x):
        return [hop(x, "y", -d) for d in (1, 2, 3)]

    def spread_h(x):
        return [hop(x, "h")]

    together = lax.optimization_barrier

    def token_part(x):
        return dot_nt(x[:, :1024], gate_weight) + dot_nt(x[:, 1024:2048], up_weight)

    mine = lax.optimization_barrier(jnp.concatenate([tokens, cotangent]))
    near, far = lax.optimization_barrier((ring(mine), ring(hop(mine, "l"))))
    near, far = ([*up, jnp.concatenate(last), *down[:0:-1]] for up, last, down in (near, far))
    f_a = select(order_a, jnp.concatenate([b[:64] for b in near]))
    g_a = select(order_a, jnp.concatenate([b[64:] for b in near]))
    f_b = select(order_b, jnp.concatenate([b[:64] for b in far]))
    g_b = select(order_b, jnp.concatenate([b[64:] for b in far]))

    crossed = hop(jnp.concatenate([f_a[256:], g_a[256:], f_b[256:], g_b[256:]]), "c")
    crossed = crossed.reshape(4, 256, 512)
    chip_a = sums(f_a[:256], g_a[:256], crossed[0], crossed[1]).reshape(2, 4, 32, 3072)
    chip_b = sums(f_b[:256], g_b[:256], crossed[2], crossed[3]).reshape(4, 2, 32, 3072)
    chip_a, chip_b = together((chip_a, chip_b))
    from_y, from_h = together((send_y(lambda d: chip_a[:, d]), send_h(lambda d: chip_b[:, d])))
    pair_a, line_b = together((add(chip_a[:, 0], from_y), add(chip_b[:, 0], from_h)))
    features, grads = jnp.concatenate([f_a, f_b]), jnp.concatenate([g_a, g_b])
    features, grads = together((features, grads))
    from_h, from_y = together((send_h(lambda d: pair_a[d]), send_y(lambda d: line_b[d])))
    act_a = activate(add(pair_a[0], from_h))
    act_b = activate(add(line_b[0], from_y))

    from_y, from_h = together((spread_y(act_a), spread_h(act_b)))
    act_a, act_b = together((jnp.concatenate([act_a] + from_y), jnp.concatenate([act_b] + from_h)))
    from_h, from_y = together((spread_h(act_a), spread_y(act_b)))
    act_a, act_b = together((jnp.concatenate([act_a] + from_h), jnp.concatenate([act_b] + from_y)))
    other_b = hop(act_b, "c")
    other_a = hop(act_a, "c")

    def far_part(x):
        x = token_part(x).astype(BF).reshape(4, 2, 32, 512).swapaxes(0, 1).reshape(256, 512)
        return hop(x, "l")

    far_own, far_other = together((far_part(act_b), far_part(other_b)))
    near_part = jnp.concatenate(
        [token_part(act_a) + far_own.astype(F32), token_part(other_a) + far_other.astype(F32)]
    )
    near_part = restore(place_a, near_part.astype(BF))
    token_grad = swap(near_part, "z").astype(F32).reshape(8, 64, 512).sum(0)
    every = jnp.concatenate([act_a, other_a, act_b, other_b])
    return (
        token_grad,
        dot_tn(features, every[:, :1024]),
        dot_tn(features, every[:, 1024:2048]),
        dot_tn(every[:, 2048:], grads),
    )


def solution(mesh):
    fine = Mesh(mesh.devices.reshape(4, 2, 2, 2, 8), ("y", "h", "c", "l", "z"))
    row, col = ("y", "h", "c"), ("l", "z")
    return jax.shard_map(
        shards,
        mesh=fine,
        in_specs=(P(col, row), P(col, row), P(row, col), P(row, col), P(col, row)),
        out_specs=(P(col, row), P(row, col), P(row, col), P(col, row)),
        check_vma=False,
    )
```

```python
import jax
import jax.numpy as jnp
from jax import lax
from jax.sharding import Mesh, PartitionSpec as P

BF = jnp.bfloat16
F16 = jnp.float16
F32 = jnp.float32
SIZES = {"y": 4, "h": 2, "c": 2, "l": 2, "z": 8}


def hop(x, axis, step=1):
    n = SIZES[axis]
    return lax.ppermute(x, axis, [(i, (i + step) % n) for i in range(n)])


def swap(x, axis):
    return lax.all_to_all(x, axis, 0, 0, tiled=True)


def ring(x, ups, downs):
    up, down = [x], [x]
    for step in range(4):
        if step < ups:
            up.append(hop(up[-1], "z", 1))
        if step < downs:
            down.append(hop(down[-1], "z", -1))
    return up + down[:0:-1]


def encode(v):
    return (v * 16.0).astype(F16)


def decode(v):
    return v.astype(F32) * (1.0 / 16.0)


def dot_nn(a, b):
    return jnp.dot(a, b, preferred_element_type=F32)


def dot_nt(a, b):
    return lax.dot_general(a, b, (((1,), (1,)), ((), ())), preferred_element_type=F32)


def dot_tn(a, b):
    return lax.dot_general(a, b, (((0,), (0,)), ((), ())), preferred_element_type=F32)


def select(order, x):
    hot = (order[:, None] == jnp.arange(x.shape[0])[None, :]).astype(BF)
    return dot_nn(hot, x).astype(BF)


def restore(order, x):
    hot = (order[:, None] == jnp.arange(x.shape[0])[None, :]).astype(BF)
    return dot_tn(hot, x).astype(BF)


def shards(tokens, cotangent, gate_weight, up_weight, down_weight):
    y, h, c, z = (lax.axis_index(a) for a in ("y", "h", "c", "z"))

    i = jnp.arange(256)
    block, low = i // 32, i % 32
    chips_a = (y + block % 4) % 4 * 2 + (h + block // 4) % 2
    chips_b = (y + block // 2) % 4 * 2 + (h + block % 2) % 2

    order_a, order_b = (
        jnp.concatenate([(z - chips) % 8 * 64 + core * 32 + low for core in (c, 1 - c)])
        for chips in (chips_a, chips_b)
    )
    place_a = jnp.concatenate([chips_a * 64 + core * 32 + low for core in (c, 1 - c)])

    gate_other, up_other, down_other = (hop(w, "c") for w in (gate_weight, up_weight, down_weight))

    def sums(f, g, f_other, g_other):
        return jnp.concatenate(
            [
                dot_nn(f, gate_weight) + dot_nn(f_other, gate_other),
                dot_nn(f, up_weight) + dot_nn(f_other, up_other),
                dot_nt(g, down_weight) + dot_nt(g_other, down_other),
            ],
            axis=1,
        )

    def activate(total):
        gate, up, hidden_grad = total[:, :1024], total[:, 1024:2048], total[:, 2048:]
        sigma = jax.nn.sigmoid(gate)
        silu_gate = gate * sigma
        hidden = (silu_gate * up).astype(BF)
        pre_gate = (hidden_grad * up * sigma * (1.0 + gate * (1.0 - sigma))).astype(BF)
        pre_up = (hidden_grad * silu_gate).astype(BF)
        return jnp.concatenate([pre_gate, pre_up, hidden], axis=1)

    def send_y(x):
        return [hop(encode(x(d)), "y", d) for d in (2, 1, 3)]

    def send_h(x):
        return [hop(encode(x(1)), "h")]

    def add(own, others):
        return own + sum(decode(other) for other in others)

    def spread_y(x):
        return [hop(x, "y", -d) for d in (1, 2, 3)]

    def spread_h(x):
        return [hop(x, "h")]

    together = lax.optimization_barrier

    def token_part(x):
        return dot_nt(x[:, :1024], gate_weight) + dot_nt(x[:, 1024:2048], up_weight)

    mine = lax.optimization_barrier(jnp.concatenate([tokens, cotangent]))
    near, far = lax.optimization_barrier((ring(mine, 4, 3), ring(hop(mine, "l"), 3, 4)))
    f_a = select(order_a, jnp.concatenate([b[:64] for b in near]))
    g_a = select(order_a, jnp.concatenate([b[64:] for b in near]))
    f_b = select(order_b, jnp.concatenate([b[:64] for b in far]))
    g_b = select(order_b, jnp.concatenate([b[64:] for b in far]))

    crossed = hop(jnp.concatenate([f_a[256:], g_a[256:], f_b[256:], g_b[256:]]), "c")
    crossed = crossed.reshape(4, 256, 512)
    chip_a = sums(f_a[:256], g_a[:256], crossed[0], crossed[1]).reshape(2, 4, 32, 3072)
    chip_b = sums(f_b[:256], g_b[:256], crossed[2], crossed[3]).reshape(4, 2, 32, 3072)
    chip_a, chip_b = together((chip_a, chip_b))
    from_y, from_h = together((send_y(lambda d: chip_a[:, d]), send_h(lambda d: chip_b[:, d])))
    pair_a, line_b = together((add(chip_a[:, 0], from_y), add(chip_b[:, 0], from_h)))
    features, grads = jnp.concatenate([f_a, f_b]), jnp.concatenate([g_a, g_b])
    features, grads = together((features, grads))
    from_h, from_y = together((send_h(lambda d: pair_a[d]), send_y(lambda d: line_b[d])))
    act_a = activate(add(pair_a[0], from_h))
    act_b = activate(add(line_b[0], from_y))

    from_y, from_h = together((spread_y(act_a), spread_h(act_b)))
    act_a, act_b = together((jnp.concatenate([act_a] + from_y), jnp.concatenate([act_b] + from_h)))
    from_h, from_y = together((spread_h(act_a), spread_y(act_b)))
    act_a, act_b = together((jnp.concatenate([act_a] + from_h), jnp.concatenate([act_b] + from_y)))
    other_b = hop(act_b, "c")
    other_a = hop(act_a, "c")

    def far_part(x):
        x = token_part(x).astype(BF).reshape(4, 2, 32, 512).swapaxes(0, 1).reshape(256, 512)
        return hop(x, "l")

    far_own, far_other = together((far_part(act_b), far_part(other_b)))
    near_part = jnp.concatenate(
        [token_part(act_a) + far_own.astype(F32), token_part(other_a) + far_other.astype(F32)]
    )
    near_part = restore(place_a, near_part.astype(BF))
    token_grad = swap(near_part, "z").astype(F32).reshape(8, 64, 512).sum(0)
    every = jnp.concatenate([act_a, other_a, act_b, other_b])
    return (
        token_grad,
        dot_tn(features, every[:, :1024]),
        dot_tn(features, every[:, 1024:2048]),
        dot_tn(every[:, 2048:], grads),
    )


def solution(mesh):
    fine = Mesh(mesh.devices.reshape(4, 2, 2, 2, 8), ("y", "h", "c", "l", "z"))
    row, col = ("y", "h", "c"), ("l", "z")
    return jax.shard_map(
        shards,
        mesh=fine,
        in_specs=(P(col, row), P(col, row), P(row, col), P(row, col), P(col, row)),
        out_specs=(P(col, row), P(row, col), P(row, col), P(col, row)),
        check_vma=False,
    )
```

```python
import jax
import jax.numpy as jnp
from jax import lax
from jax.sharding import Mesh, PartitionSpec as P

BF = jnp.bfloat16
F16 = jnp.float16
F32 = jnp.float32
SIZES = {"y": 4, "h": 2, "c": 2, "l": 2, "z": 8}


def hop(x, axis, step=1):
    n = SIZES[axis]
    return lax.ppermute(x, axis, [(i, (i + step) % n) for i in range(n)])


def swap(x, axis):
    return lax.all_to_all(x, axis, 0, 0, tiled=True)


def ring(x, ups, downs):
    up, down = [x], [x]
    for step in range(4):
        if step < ups:
            up.append(hop(up[-1], "z", 1))
        if step < downs:
            down.append(hop(down[-1], "z", -1))
    return up + down[:0:-1]


def encode(v):
    return (v * 16.0).astype(F16)


def decode(v):
    return v.astype(F32) * (1.0 / 16.0)


def dot_nn(a, b):
    return jnp.dot(a, b, preferred_element_type=F32)


def dot_nt(a, b):
    return lax.dot_general(a, b, (((1,), (1,)), ((), ())), preferred_element_type=F32)


def dot_tn(a, b):
    return lax.dot_general(a, b, (((0,), (0,)), ((), ())), preferred_element_type=F32)


def select(order, x):
    hot = (order[:, None] == jnp.arange(x.shape[0])[None, :]).astype(BF)
    return dot_nn(hot, x).astype(BF)


def restore(order, x):
    hot = (order[:, None] == jnp.arange(x.shape[0])[None, :]).astype(BF)
    return dot_tn(hot, x).astype(BF)


def shards(tokens, cotangent, gate_weight, up_weight, down_weight):
    y, h, c, z = (lax.axis_index(a) for a in ("y", "h", "c", "z"))

    i = jnp.arange(256)
    block, low = i // 32, i % 32
    chips_b = (y + block % 4) % 4 * 2 + (h + block // 4) % 2
    chips_a = (y + block // 2) % 4 * 2 + (h + block % 2) % 2

    order_a, order_b = (
        jnp.concatenate([(z - chips) % 8 * 64 + core * 32 + low for core in (c, 1 - c)])
        for chips in (chips_a, chips_b)
    )
    place_a = jnp.concatenate([chips_a * 64 + core * 32 + low for core in (c, 1 - c)])

    gate_other, up_other, down_other = (hop(w, "c") for w in (gate_weight, up_weight, down_weight))

    def sums(f, g, f_other, g_other):
        return jnp.concatenate(
            [
                dot_nn(f, gate_weight) + dot_nn(f_other, gate_other),
                dot_nn(f, up_weight) + dot_nn(f_other, up_other),
                dot_nt(g, down_weight) + dot_nt(g_other, down_other),
            ],
            axis=1,
        )

    def activate(total):
        gate, up, hidden_grad = total[:, :1024], total[:, 1024:2048], total[:, 2048:]
        sigma = jax.nn.sigmoid(gate)
        silu_gate = gate * sigma
        hidden = (silu_gate * up).astype(BF)
        pre_gate = (hidden_grad * up * sigma * (1.0 + gate * (1.0 - sigma))).astype(BF)
        pre_up = (hidden_grad * silu_gate).astype(BF)
        return jnp.concatenate([pre_gate, pre_up, hidden], axis=1)

    def send_y(x):
        return [hop(encode(x(d)), "y", d) for d in (2, 1, 3)]

    def add(own, others):
        return own + sum(decode(other) for other in others)

    def spread_y(x):
        return [hop(x, "y", -d) for d in (1, 2, 3)]

    together = lax.optimization_barrier

    def token_part(x):
        return dot_nt(x[:, :1024], gate_weight) + dot_nt(x[:, 1024:2048], up_weight)

    mine = lax.optimization_barrier(jnp.concatenate([tokens, cotangent]))
    near, far = lax.optimization_barrier((ring(mine, 4, 3), ring(hop(mine, "l"), 3, 4)))
    f_a = select(order_a, jnp.concatenate([b[:64] for b in near]))
    g_a = select(order_a, jnp.concatenate([b[64:] for b in near]))
    f_b = select(order_b, jnp.concatenate([b[:64] for b in far]))
    g_b = select(order_b, jnp.concatenate([b[64:] for b in far]))

    crossed = hop(jnp.concatenate([f_a[256:], g_a[256:], f_b[256:], g_b[256:]]), "c")
    crossed = crossed.reshape(4, 256, 512)
    chip_a = sums(f_a[:256], g_a[:256], crossed[0], crossed[1]).reshape(4, 64, 3072)
    chip_b = sums(f_b[:256], g_b[:256], crossed[2], crossed[3]).reshape(2, 128, 3072)
    chip_a, chip_b = together((chip_a, chip_b))
    from_y, from_h = together((send_y(lambda d: chip_a[d]), hop(encode(chip_b[1]), "h")))
    pair_a, line_b = together((add(chip_a[0], from_y), chip_b[0] + decode(from_h)))
    features, grads = jnp.concatenate([f_a, f_b]), jnp.concatenate([g_a, g_b])
    features, grads = together((features, grads))
    line_b = line_b.reshape(4, 32, 3072)
    from_h, from_y = together((hop(encode(pair_a), "h"), send_y(lambda d: line_b[d])))
    act_a = activate(pair_a + decode(jnp.concatenate([from_h[32:], from_h[:32]])))
    act_b = activate(add(line_b[0], from_y))

    act_b = together(jnp.concatenate([act_b] + spread_y(act_b)))
    from_y, from_h = together((spread_y(act_a), hop(act_b, "h")))
    act_a = jnp.concatenate([act_a] + from_y)
    act_a, act_b = together((act_a, jnp.concatenate([act_b, from_h])))
    other_b = hop(act_b, "c")
    other_a = hop(act_a, "c")

    def far_part(x):
        x = token_part(x).astype(BF).reshape(2, 4, 32, 512).swapaxes(0, 1).reshape(256, 512)
        return hop(x, "l")

    far_own, far_other = together((far_part(act_b), far_part(other_b)))
    near_part = jnp.concatenate(
        [token_part(act_a) + far_own.astype(F32), token_part(other_a) + far_other.astype(F32)]
    )
    near_part = restore(place_a, near_part.astype(BF))
    token_grad = swap(near_part, "z").astype(F32).reshape(8, 64, 512).sum(0)
    every = jnp.concatenate([act_a, other_a, act_b, other_b])
    return (
        token_grad,
        dot_tn(features, every[:, :1024]),
        dot_tn(features, every[:, 1024:2048]),
        dot_tn(every[:, 2048:], grads),
    )


def solution(mesh):
    fine = Mesh(mesh.devices.reshape(4, 2, 2, 2, 8), ("y", "h", "c", "l", "z"))
    row, col = ("y", "h", "c"), ("l", "z")
    return jax.shard_map(
        shards,
        mesh=fine,
        in_specs=(P(col, row), P(col, row), P(row, col), P(row, col), P(col, row)),
        out_specs=(P(col, row), P(row, col), P(row, col), P(col, row)),
        check_vma=False,
    )
```

```python
import jax
import jax.numpy as jnp
from jax import lax
from jax.sharding import Mesh, PartitionSpec as P

BF = jnp.bfloat16
F16 = jnp.float16
F32 = jnp.float32
SIZES = {"y": 4, "h": 2, "c": 2, "l": 2, "z": 8}


def hop(x, axis, step=1):
    n = SIZES[axis]
    return lax.ppermute(x, axis, [(i, (i + step) % n) for i in range(n)])


def swap(x, axis):
    return lax.all_to_all(x, axis, 0, 0, tiled=True)


def ring(x, ups, downs):
    up, down = [x], [x]
    for step in range(4):
        if step < ups:
            up.append(hop(up[-1], "z", 1))
        if step < downs:
            down.append(hop(down[-1], "z", -1))
    return up + down[:0:-1]


def encode(v):
    return (v * 16.0).astype(F16)


def decode(v):
    return v.astype(F32) * (1.0 / 16.0)


def dot_nn(a, b):
    return jnp.dot(a, b, preferred_element_type=F32)


def dot_nt(a, b):
    return lax.dot_general(a, b, (((1,), (1,)), ((), ())), preferred_element_type=F32)


def dot_tn(a, b):
    return lax.dot_general(a, b, (((0,), (0,)), ((), ())), preferred_element_type=F32)


def select(order, x):
    hot = (order[:, None] == jnp.arange(x.shape[0])[None, :]).astype(BF)
    return dot_nn(hot, x).astype(BF)


def restore(order, x):
    hot = (order[:, None] == jnp.arange(x.shape[0])[None, :]).astype(BF)
    return dot_tn(hot, x).astype(BF)


def shards(tokens, cotangent, gate_weight, up_weight, down_weight):
    y, h, c, z = (lax.axis_index(a) for a in ("y", "h", "c", "z"))

    i = jnp.arange(256)
    block, low = i // 32, i % 32
    chips_b = (y + block % 4) % 4 * 2 + (h + block // 4) % 2
    chips_a = (y + block // 2) % 4 * 2 + (h + block % 2) % 2

    order_a, order_b = (
        jnp.concatenate([(z - chips) % 8 * 64 + core * 32 + low for core in (c, 1 - c)])
        for chips in (chips_a, chips_b)
    )
    place_a = jnp.concatenate([chips_a * 64 + core * 32 + low for core in (c, 1 - c)])

    gate_up_other = hop(jnp.concatenate([gate_weight, up_weight]), "c")
    gate_other, up_other = gate_up_other[:512], gate_up_other[512:]
    down_other = hop(down_weight, "c")

    def sums(f, g, f_other, g_other):
        return jnp.concatenate(
            [
                dot_nn(f, gate_weight) + dot_nn(f_other, gate_other),
                dot_nn(f, up_weight) + dot_nn(f_other, up_other),
                dot_nt(g, down_weight) + dot_nt(g_other, down_other),
            ],
            axis=1,
        )

    def activate(total):
        gate, up, hidden_grad = total[:, :1024], total[:, 1024:2048], total[:, 2048:]
        sigma = jax.nn.sigmoid(gate)
        silu_gate = gate * sigma
        hidden = (silu_gate * up).astype(BF)
        pre_gate = (hidden_grad * up * sigma * (1.0 + gate * (1.0 - sigma))).astype(BF)
        pre_up = (hidden_grad * silu_gate).astype(BF)
        return jnp.concatenate([pre_gate, pre_up, hidden], axis=1)

    def send_y(x):
        return [hop(encode(x(d)), "y", d) for d in (2, 1, 3)]

    def add(own, others):
        return own + sum(decode(other) for other in others)

    def spread_y(x):
        return [hop(x, "y", -d) for d in (1, 2, 3)]

    together = lax.optimization_barrier

    def token_part(x):
        return dot_nt(x[:, :1024], gate_weight) + dot_nt(x[:, 1024:2048], up_weight)

    mine = lax.optimization_barrier(jnp.concatenate([tokens, cotangent]))
    near, far = lax.optimization_barrier((ring(mine, 4, 3), ring(hop(mine, "l"), 3, 4)))
    f_a = select(order_a, jnp.concatenate([b[:64] for b in near]))
    g_a = select(order_a, jnp.concatenate([b[64:] for b in near]))
    f_b = select(order_b, jnp.concatenate([b[:64] for b in far]))
    g_b = select(order_b, jnp.concatenate([b[64:] for b in far]))

    crossed = hop(jnp.concatenate([f_a[256:], g_a[256:], f_b[256:], g_b[256:]]), "c")
    crossed = crossed.reshape(4, 256, 512)
    chip_a = sums(f_a[:256], g_a[:256], crossed[0], crossed[1]).reshape(4, 64, 3072)
    chip_b = sums(f_b[:256], g_b[:256], crossed[2], crossed[3]).reshape(2, 128, 3072)
    chip_a, chip_b = together((chip_a, chip_b))
    from_y, from_h = together((send_y(lambda d: chip_a[d]), hop(encode(chip_b[1]), "h")))
    pair_a, line_b = together((add(chip_a[0], from_y), chip_b[0] + decode(from_h)))
    features, grads = jnp.concatenate([f_a, f_b]), jnp.concatenate([g_a, g_b])
    features, grads = together((features, grads))
    line_b = line_b.reshape(4, 32, 3072)
    from_h, from_y = together((hop(encode(pair_a), "h"), send_y(lambda d: line_b[d])))
    act_a = activate(pair_a + decode(jnp.concatenate([from_h[32:], from_h[:32]])))
    act_b = activate(add(line_b[0], from_y))

    act_b = together(jnp.concatenate([act_b] + spread_y(act_b)))
    from_y, from_h = together((spread_y(act_a), hop(act_b, "h")))
    act_a = jnp.concatenate([act_a] + from_y)
    act_a, act_b = together((act_a, jnp.concatenate([act_b, from_h])))
    other_b = hop(act_b, "c")
    other_a = hop(act_a, "c")

    def far_part(x):
        x = token_part(x).astype(BF).reshape(2, 4, 32, 512).swapaxes(0, 1).reshape(256, 512)
        return hop(x, "l")

    far_own, far_other = together((far_part(act_b), far_part(other_b)))
    near_part = jnp.concatenate(
        [token_part(act_a) + far_own.astype(F32), token_part(other_a) + far_other.astype(F32)]
    )
    near_part = restore(place_a, near_part.astype(BF))
    token_grad = swap(near_part, "z").astype(F32).reshape(8, 64, 512).sum(0)
    every = jnp.concatenate([act_a, other_a, act_b, other_b])
    return (
        token_grad,
        dot_tn(features, every[:, :1024]),
        dot_tn(features, every[:, 1024:2048]),
        dot_tn(every[:, 2048:], grads),
    )


def solution(mesh):
    fine = Mesh(mesh.devices.reshape(4, 2, 2, 2, 8), ("y", "h", "c", "l", "z"))
    row, col = ("y", "h", "c"), ("l", "z")
    return jax.shard_map(
        shards,
        mesh=fine,
        in_specs=(P(col, row), P(col, row), P(row, col), P(row, col), P(col, row)),
        out_specs=(P(col, row), P(row, col), P(row, col), P(col, row)),
        check_vma=False,
    )
```
